32 devices in a mesh: fsdp: 8 (over y, x, core), dp: 4 (over z).
Axes of the slice: x: 2, y: 2, z: 4, core: 2. Of those that a mesh axis runs over, the one named last changes fastest.
Arguments:
- grad_out: bfloat16 [4096, 8192], P('dp', 'fsdp'), may hold values from -6 to 6
- inputs: bfloat16 [4096, 8192], P('dp', 'fsdp'), may hold values from -6 to 6
- gate_pre: bfloat16 [4096, 28672], P('dp', 'fsdp'), may hold values from -8 to 8
- down_weight: bfloat16 [28672, 8192], P('fsdp', 'dp'), may hold values from -0.0625 to 0.0625
- input_adapter_factor: bfloat16 [8192, 128], P('fsdp'), may hold values from -0.0625 to 0.0625
- adapter_second: bfloat16 [128, 28672], P(None, 'fsdp'), may hold values from -0.03125 to 0.03125
- sketch_model: int32 [8192, 64], P('fsdp'), may hold values from -1 to 1, as said below
- sketch_hidden: int32 [28672, 64], P('fsdp'), may hold values from -1 to 1, as said below
- mixer_first: int32 [128, 128], replicated, may hold values from -1 to 1, as said below
- second_sign_mixer: int32 [128, 128], replicated, may hold values from -1 to 1, as said below
Outputs:
- features: float32 [16, 8192], P('dp')
- scores: float32 [16], P('dp')
The draws below stay inside these ranges and needn't reach their ends.
Inputs may be any that keep to these rules, and one draw needn't show every extreme that they name: `sketch_model`: every entry is -1 or +1. `sketch_hidden`: every entry is -1 or +1. `mixer_first`: every entry is -1 or +1. `second_sign_mixer`: every entry is -1 or +1.
All inputs are finite; a program needn't handle non-finite values.
Results may differ from the reference program's by a relative error of at most 0.0039.
Values may be sent and summed in bfloat16 or wider, within the bound.
A program may use at most 256 MiB of HBM per device.

```python
import jax
import jax.numpy as jnp
from jax import lax

D = 8192
FF = 28672
RANK = 128
K1 = 64
K2 = 128
SEQ = 256
TOKENS = 4096


def signs_from(key, rows, cols):
    return (2 * jax.random.randint(key, (rows, cols), 0, 2) - 1).astype(jnp.int32)


def draw_sketch_model(key, part):
    key = jax.random.fold_in(key, 11)
    return signs_from(key, D, K1)


def draw_sketch_hidden(key, part):
    key = jax.random.fold_in(key, 12)
    return signs_from(key, FF, K1)


def draw_mixer_first(key, part):
    key = jax.random.fold_in(key, 13)
    return signs_from(key, RANK, K2)


def draw_second_sign_mixer(key, part):
    key = jax.random.fold_in(key, 14)
    return signs_from(key, RANK, K2)


def block_scale(stream_key, extent, cuts, smallest, high):
    def one(position, blocks):
        heights = jax.random.uniform(jax.random.fold_in(jax.random.fold_in(stream_key, 6), position), (blocks,), jnp.float32, smallest / len(cuts), high / len(cuts))
        return jnp.repeat(jnp.exp(heights), extent[position] // blocks).reshape((-1,) + (1,) * (len(extent) - position - 1))

    factor_of = one(*cuts[0])
    for cut in cuts[1:]:
        factor_of = factor_of * one(*cut)
    return factor_of


def bell_draw(key, dims, width, bound, pieces=(), kind=jnp.bfloat16):
    result = width * jax.random.normal(key, dims, jnp.float32)
    if pieces:
        result = result * block_scale(key, dims, pieces, -0.22, 0.18)
    return jnp.clip(result, -bound, bound).astype(kind)


def setup_inputs(seed: int = 0) -> dict:
    key_of = jax.random.split(jax.random.key(seed), 11)
    grad_out = bell_draw(key_of[0], (TOKENS, D), 1.0, 6.0, ((0, 4), (1, 8)))
    inputs = bell_draw(key_of[1], (TOKENS, D), 1.0, 6.0, ((0, 4), (1, 8)))
    gate_pre = bell_draw(key_of[2], (TOKENS, FF), 1.5, 8.0, ((0, 4), (1, 8)))
    down_weight = bell_draw(key_of[3], (FF, D), D ** -0.5, 0.0625, ((0, 8), (1, 4)))
    input_adapter_factor = bell_draw(key_of[4], (D, RANK), D ** -0.5, 0.0625, ((0, 8),))
    adapter_second = bell_draw(key_of[5], (RANK, FF), FF ** -0.5, 0.03125, ((1, 8),))
    sketch_model = draw_sketch_model(jax.random.fold_in(key_of[10], 71), 0)
    sketch_hidden = draw_sketch_hidden(jax.random.fold_in(key_of[10], 71), 0)
    mixer_first = draw_mixer_first(jax.random.fold_in(key_of[10], 71), 0)
    second_sign_mixer = draw_second_sign_mixer(jax.random.fold_in(key_of[10], 71), 0)
    return dict(grad_out=grad_out, inputs=inputs, gate_pre=gate_pre, down_weight=down_weight, input_adapter_factor=input_adapter_factor, adapter_second=adapter_second, sketch_model=sketch_model, sketch_hidden=sketch_hidden, mixer_first=mixer_first, second_sign_mixer=second_sign_mixer)


def reference(grad_out, inputs, gate_pre, down_weight, input_adapter_factor, adapter_second, sketch_model, sketch_hidden, mixer_first, second_sign_mixer):
    upstream = jnp.dot(grad_out, down_weight.T, preferred_element_type=jnp.float32)
    scaled_result = (upstream * jax.nn.silu(gate_pre.astype(jnp.float32))).astype(jnp.bfloat16)
    low_rank_input = jnp.dot(inputs, input_adapter_factor, preferred_element_type=jnp.float32).astype(jnp.bfloat16)
    back = jnp.dot(scaled_result, adapter_second.T, preferred_element_type=jnp.float32)
    left_model = jnp.dot(inputs, sketch_model.astype(jnp.bfloat16), preferred_element_type=jnp.float32)
    left_hidden = jnp.dot(scaled_result, sketch_hidden.astype(jnp.bfloat16), preferred_element_type=jnp.float32)
    right_first = jnp.dot(back, mixer_first.astype(jnp.float32), precision=lax.Precision.HIGHEST)
    second_right_factor = jnp.dot(low_rank_input, second_sign_mixer.astype(jnp.bfloat16), preferred_element_type=jnp.float32)
    count = grad_out.shape[0] // SEQ
    left_model = left_model.reshape(count, SEQ, K1)
    left_hidden = left_hidden.reshape(count, SEQ, K1)
    right_first = right_first.reshape(count, SEQ, K2)
    second_right_factor = second_right_factor.reshape(count, SEQ, K2)
    projected = jnp.einsum('esa,esb->eab', left_hidden, second_right_factor, precision=lax.Precision.HIGHEST)
    projected = projected + jnp.einsum('esa,esb->eab', left_model, right_first, precision=lax.Precision.HIGHEST)
    projected = projected.reshape(count, K1 * K2)
    features = projected * lax.rsqrt(lax.optimization_barrier(jnp.mean(projected * projected, axis=1, keepdims=True)) + 1e-06)
    centre = lax.optimization_barrier(jnp.sum(features, axis=0)) / count
    scores = jnp.dot(features, centre, precision=lax.Precision.HIGHEST) / (K1 * K2 * jnp.sqrt(jnp.mean(centre * centre) + 1e-06))
    return (features, scores)
```

```python
import jax
import jax.numpy as jnp
from jax import lax
from jax.sharding import PartitionSpec as P

K1 = 64
K2 = 128
SEQ = 256
CHUNKS = 14
LAG = 2
GROUP = 2


def contract_last(left, right):
    return lax.dot_general(
        left, right, (((1,), (1,)), ((), ())), preferred_element_type=jnp.float32
    )


def body(
    grad_out,
    inputs,
    gate_pre,
    down_weight,
    input_adapter_factor,
    adapter_second,
    sketch_model,
    sketch_hidden,
    mixer_first,
    second_sign_mixer,
):
    z = lax.axis_index("dp")
    planes = lax.axis_size("dp")
    ranks = lax.axis_size("fsdp")
    outer = (z == 0) | (z == 3)
    low = z < 2
    tokens, hidden = gate_pre.shape
    width = hidden // CHUNKS
    span = width * GROUP
    rank = adapter_second.shape[0]

    own = [gate_pre[:, i * width : (i + 1) * width] for i in range(CHUNKS)]

    rows = lax.all_to_all(grad_out, "fsdp", 0, 1, tiled=True)
    rows = lax.all_to_all(rows, "dp", 1, 0, tiled=True)
    rows = rows.reshape(planes, tokens // ranks, down_weight.shape[1])

    def gathered(block):
        piece = lax.dynamic_index_in_dim(rows, block, 0, keepdims=False)
        return lax.all_gather(piece, "fsdp", axis=0, tiled=True)

    block_a = z ^ 1
    block_c = jnp.where(low, 2, 1)
    block_d = jnp.where(low, 3, 0)
    grad_a = gathered(block_a)
    grad_c = gathered(block_c)
    grad_b = gathered(z)
    grad_d = gathered(block_d)

    model_factors = jnp.concatenate(
        [input_adapter_factor, sketch_model.astype(jnp.bfloat16)], axis=1
    )
    model_side = jnp.dot(inputs, model_factors, preferred_element_type=jnp.float32)
    model_side = lax.psum(model_side, "fsdp")
    second_right = jnp.dot(
        model_side[:, :rank].astype(jnp.bfloat16),
        second_sign_mixer.astype(jnp.bfloat16),
        preferred_element_type=jnp.float32,
    )
    model_side = jnp.concatenate([second_right, model_side[:, rank:]], axis=1)
    model_side = lax.all_gather(model_side, "dp", axis=0, tiled=True)

    hidden_factors = jnp.concatenate(
        [adapter_second, sketch_hidden.astype(jnp.bfloat16).T], axis=0
    )

    def silu(v):
        return jax.nn.silu(v.astype(jnp.float32))

    def upstream(grad, group):
        return contract_last(grad, down_weight[group * span : (group + 1) * span])

    def sketched(scaled, group):
        return contract_last(scaled, hidden_factors[:, group * span : (group + 1) * span])

    def joined(pieces):
        return jnp.concatenate(pieces, axis=1)

    steps = 2 * CHUNKS + LAG
    from_left, from_right = [], []
    partial_out = [None] * CHUNKS
    total_a = total_b = total_c = total_d = 0.0

    def near(s):
        return jnp.where(low, from_left[s], from_right[s])

    def far(s):
        ahead = jnp.where(low, from_right[s], from_left[s])
        late = jnp.where(low, from_right[s + LAG], from_left[s + LAG])
        return jnp.where(outer, late, ahead)

    def to_send(s, received, first, second, third):
        if s < CHUNKS:
            value = own[s]
        elif s < 2 * CHUNKS:
            value = jnp.where(z == first, partial_out[s - CHUNKS], received[s - CHUNKS])
        else:
            return received[s - LAG]
        if s >= LAG:
            value = jnp.where(z == third, received[s - LAG], value)
        return value

    for s in range(steps):
        if CHUNKS <= s < 2 * CHUNKS and s % GROUP == 0:
            group = (s - CHUNKS) // GROUP
            gate = joined([near(group * GROUP + k) for k in range(GROUP)])
            up = upstream(grad_a, group)
            scaled = jnp.where(outer, up, up * silu(gate)).astype(jnp.bfloat16)
            total_a = total_a + sketched(scaled, group)
            for k in range(GROUP):
                partial_out[group * GROUP + k] = scaled[:, k * width : (k + 1) * width]
        pairs = []
        if s < 2 * CHUNKS:
            pairs += [(0, 1), (1, 2)]
        if s >= LAG:
            pairs += [(2, 3)]
        going_right = to_send(s, from_left, 0, 1, 2)
        going_left = to_send(s, from_right, 3, 2, 1)
        from_left.append(lax.ppermute(going_right, "dp", pairs))
        from_right.append(lax.ppermute(going_left, "dp", [(3 - a, 3 - b) for a, b in pairs]))

    for group in range(CHUNKS // GROUP):
        places = [group * GROUP + k for k in range(GROUP)]
        scaled = (upstream(grad_c, group) * silu(joined([far(i) for i in places]))).astype(
            jnp.bfloat16
        )
        total_c = total_c + sketched(scaled, group)
        extra = joined([near(CHUNKS + i) for i in places]).astype(jnp.float32)
        up = upstream(grad_b, group) + jnp.where(outer, 0.0, extra)
        gate = gate_pre[:, group * span : (group + 1) * span]
        scaled = (up * silu(gate)).astype(jnp.bfloat16)
        total_b = total_b + sketched(scaled, group)
        scaled = (
            upstream(grad_d, group) * silu(joined([far(CHUNKS + i) for i in places]))
        ).astype(jnp.bfloat16)
        total_d = total_d + sketched(scaled, group)

    sums = jnp.zeros((planes, tokens, rank + K1), jnp.float32)
    for block, total in (
        (block_a, jnp.where(outer, 0.0, total_a)),
        (z, total_b),
        (block_c, total_c),
        (block_d, total_d),
    ):
        sums = lax.dynamic_update_index_in_dim(sums, total, block, 0)

    count = tokens // SEQ
    sums = sums.reshape(planes * count, SEQ, rank + K1)
    model_side = model_side.reshape(planes * count, SEQ, K2 + K1)
    back, left_hidden = sums[..., :rank], sums[..., rank:]
    second_right, left_model = model_side[..., :K2], model_side[..., K2:]
    projected = jnp.einsum(
        "esa,esb->eab", left_hidden, second_right, precision=lax.Precision.HIGHEST
    )
    crossed = jnp.einsum("esa,esr->ear", left_model, back, precision=lax.Precision.HIGHEST)
    projected = projected + jnp.einsum(
        "ear,rb->eab",
        crossed,
        mixer_first.astype(jnp.float32),
        precision=lax.Precision.HIGHEST,
    )
    projected = lax.psum(projected, ("fsdp", "dp")).reshape(planes * count, K1 * K2)
    features = projected * lax.rsqrt(jnp.mean(projected * projected, axis=1, keepdims=True) + 1e-06)
    centre = jnp.sum(features, axis=0) / (planes * count)
    features = lax.dynamic_slice_in_dim(features, z * count, count, 0)
    scores = jnp.dot(features, centre, precision=lax.Precision.HIGHEST) / (
        K1 * K2 * jnp.sqrt(jnp.mean(centre * centre) + 1e-06)
    )
    return (features, scores)


def solution(mesh):
    placed = (
        P("dp", "fsdp"),
        P("dp", "fsdp"),
        P("dp", "fsdp"),
        P("fsdp", "dp"),
        P("fsdp", None),
        P(None, "fsdp"),
        P("fsdp", None),
        P("fsdp", None),
        P(),
        P(),
    )
    return jax.shard_map(
        body, mesh=mesh, in_specs=placed, out_specs=(P("dp", None), P("dp")), check_vma=False
    )
```

```python
import jax
import jax.numpy as jnp
from jax import lax
from jax.sharding import PartitionSpec as P

K1 = 64
K2 = 128
SEQ = 256
CHUNKS = 4


def contract_last(left, right):
    return lax.dot_general(
        left, right, (((1,), (1,)), ((), ())), preferred_element_type=jnp.float32
    )


def body(
    grad_out,
    inputs,
    gate_pre,
    down_weight,
    input_adapter_factor,
    adapter_second,
    sketch_model,
    sketch_hidden,
    mixer_first,
    second_sign_mixer,
):
    z = lax.axis_index("dp")
    planes = lax.axis_size("dp")
    ranks = lax.axis_size("fsdp")
    outer = (z == 0) | (z == 3)
    low = z < 2
    tokens, hidden = gate_pre.shape
    width = hidden // CHUNKS
    span = width
    rank = adapter_second.shape[0]

    own = [gate_pre[:, i * width : (i + 1) * width] for i in range(CHUNKS)]

    inward = [(0, 1), (3, 2)]
    across = [(1, 2), (2, 1)]
    outward = [(1, 0), (2, 3)]
    near = [lax.ppermute(v, "dp", inward) for v in own]
    far_inner = [lax.ppermute(v, "dp", across) for v in own]
    grad_out, near[0], far_inner[0] = lax.optimization_barrier(
        (grad_out, near[0], far_inner[0])
    )
    far_outer = [lax.ppermute(v, "dp", outward) for v in far_inner]
    last_inner = [lax.ppermute(v, "dp", across) for v in near]
    last_outer = [lax.ppermute(v, "dp", outward) for v in last_inner]

    rows = lax.all_to_all(grad_out, "fsdp", 0, 1, tiled=True)
    rows = lax.all_to_all(rows, "dp", 1, 0, tiled=True)
    rows = rows.reshape(planes, tokens // ranks, down_weight.shape[1])

    def gathered(block):
        piece = lax.dynamic_index_in_dim(rows, block, 0, keepdims=False)
        return lax.all_gather(piece, "fsdp", axis=0, tiled=True)

    block_a = z ^ 1
    block_c = jnp.where(low, 2, 1)
    block_d = jnp.where(low, 3, 0)
    grad_a = gathered(block_a)
    grad_c = gathered(block_c)
    grad_b = gathered(z)
    grad_d = gathered(block_d)

    model_factors = jnp.concatenate(
        [input_adapter_factor, sketch_model.astype(jnp.bfloat16)], axis=1
    )
    model_side = jnp.dot(inputs, model_factors, preferred_element_type=jnp.float32)
    model_side = lax.psum(model_side, "fsdp")
    second_right = jnp.dot(
        model_side[:, :rank].astype(jnp.bfloat16),
        second_sign_mixer.astype(jnp.bfloat16),
        preferred_element_type=jnp.float32,
    )
    model_side = jnp.concatenate([second_right, model_side[:, rank:]], axis=1)
    model_side = lax.all_gather(model_side, "dp", axis=0, tiled=True)

    hidden_factors = jnp.concatenate(
        [adapter_second, sketch_hidden.astype(jnp.bfloat16).T], axis=0
    )

    def silu(v):
        return jax.nn.silu(v.astype(jnp.float32))

    def upstream(grad, group):
        return contract_last(grad, down_weight[group * span : (group + 1) * span])

    def sketched(scaled, group):
        return contract_last(scaled, hidden_factors[:, group * span : (group + 1) * span])

    total_a = total_b = total_c = total_d = 0.0
    neighbour = []
    for i in range(CHUNKS):
        up = upstream(grad_a, i)
        scaled = jnp.where(outer, up, up * silu(near[i])).astype(jnp.bfloat16)
        total_a = total_a + sketched(scaled, i)
        neighbour.append(lax.ppermute(scaled, "dp", inward))
    for i in range(CHUNKS):
        gate = jnp.where(outer, far_outer[i], far_inner[i])
        scaled = (upstream(grad_c, i) * silu(gate)).astype(jnp.bfloat16)
        total_c = total_c + sketched(scaled, i)
    for i in range(CHUNKS):
        up = upstream(grad_b, i) + jnp.where(outer, 0.0, neighbour[i].astype(jnp.float32))
        scaled = (up * silu(own[i])).astype(jnp.bfloat16)
        total_b = total_b + sketched(scaled, i)
        gate = jnp.where(outer, last_outer[i], last_inner[i])
        scaled = (upstream(grad_d, i) * silu(gate)).astype(jnp.bfloat16)
        total_d = total_d + sketched(scaled, i)

    total_a = jnp.where(outer, 0.0, total_a)
    low_pair = jnp.stack([jnp.where(z == 0, total_b, total_a), jnp.where(z == 0, total_a, total_b)])
    high_pair = jnp.stack([jnp.where(z == 2, total_b, total_a), jnp.where(z == 2, total_a, total_b)])
    others = jnp.stack([jnp.where(low, total_c, total_d), jnp.where(low, total_d, total_c)])
    sums = jnp.concatenate(
        [jnp.where(low, low_pair, others), jnp.where(low, others, high_pair)], axis=0
    )

    count = tokens // SEQ
    sums = sums.reshape(planes * count, SEQ, rank + K1)
    model_side = model_side.reshape(planes * count, SEQ, K2 + K1)
    back, left_hidden = sums[..., :rank], sums[..., rank:]
    second_right, left_model = model_side[..., :K2], model_side[..., K2:]
    projected = jnp.einsum(
        "esa,esb->eab", left_hidden, second_right, precision=lax.Precision.HIGHEST
    )
    crossed = jnp.einsum("esa,esr->ear", left_model, back, precision=lax.Precision.HIGHEST)
    projected = projected + jnp.einsum(
        "ear,rb->eab",
        crossed,
        mixer_first.astype(jnp.float32),
        precision=lax.Precision.HIGHEST,
    )
    projected = projected.reshape(planes, count, K1 * K2)
    projected = lax.all_to_all(projected, "dp", 0, 0, tiled=True)
    projected = lax.psum(jnp.sum(projected, axis=0), "fsdp")
    features = projected * lax.rsqrt(jnp.mean(projected * projected, axis=1, keepdims=True) + 1e-06)
    centre = jnp.sum(lax.all_gather(jnp.sum(features, axis=0), "dp"), axis=0) / (planes * count)
    scores = jnp.dot(features, centre, precision=lax.Precision.HIGHEST) / (
        K1 * K2 * jnp.sqrt(jnp.mean(centre * centre) + 1e-06)
    )
    return (features, scores)


def solution(mesh):
    placed = (
        P("dp", "fsdp"),
        P("dp", "fsdp"),
        P("dp", "fsdp"),
        P("fsdp", "dp"),
        P("fsdp", None),
        P(None, "fsdp"),
        P("fsdp", None),
        P("fsdp", None),
        P(),
        P(),
    )
    return jax.shard_map(
        body, mesh=mesh, in_specs=placed, out_specs=(P("dp", None), P("dp")), check_vma=False
    )
```

```python
import jax
import jax.numpy as jnp
from jax import lax
from jax.sharding import PartitionSpec as P

K1 = 64
K2 = 128
SEQ = 256
CHUNKS = 2


def contract_last(left, right):
    return lax.dot_general(
        left, right, (((1,), (1,)), ((), ())), preferred_element_type=jnp.float32
    )


def body(
    grad_out,
    inputs,
    gate_pre,
    down_weight,
    input_adapter_factor,
    adapter_second,
    sketch_model,
    sketch_hidden,
    mixer_first,
    second_sign_mixer,
):
    z = lax.axis_index("dp")
    planes = lax.axis_size("dp")
    ranks = lax.axis_size("fsdp")
    outer = (z == 0) | (z == 3)
    low = z < 2
    tokens, hidden = gate_pre.shape
    width = hidden // CHUNKS
    span = width
    rank = adapter_second.shape[0]

    own = [gate_pre[:, i * width : (i + 1) * width] for i in range(CHUNKS)]

    inward = [(0, 1), (3, 2)]
    across = [(1, 2), (2, 1)]
    outward = [(1, 0), (2, 3)]
    near = [lax.ppermute(v, "dp", inward) for v in own]
    far_inner = [lax.ppermute(v, "dp", across) for v in own]
    grad_out, near[0], far_inner[0] = lax.optimization_barrier(
        (grad_out, near[0], far_inner[0])
    )
    far_outer = [lax.ppermute(v, "dp", outward) for v in far_inner]
    last_inner = [lax.ppermute(v, "dp", across) for v in near]
    last_outer = [lax.ppermute(v, "dp", outward) for v in last_inner]

    rows = lax.all_to_all(grad_out, "fsdp", 0, 1, tiled=True)
    rows = lax.all_to_all(rows, "dp", 1, 0, tiled=True)
    rows = rows.reshape(planes, tokens // ranks, down_weight.shape[1])

    def gathered(block):
        piece = lax.dynamic_index_in_dim(rows, block, 0, keepdims=False)
        return lax.all_gather(piece, "fsdp", axis=0, tiled=True)

    block_a = z ^ 1
    block_c = jnp.where(low, 2, 1)
    block_d = jnp.where(low, 3, 0)
    grad_a = gathered(block_a)
    grad_c = gathered(block_c)
    grad_b = gathered(z)
    grad_d = gathered(block_d)

    model_factors = jnp.concatenate(
        [input_adapter_factor, sketch_model.astype(jnp.bfloat16)], axis=1
    )
    model_side = jnp.dot(inputs, model_factors, preferred_element_type=jnp.float32)
    model_side = lax.psum(model_side, "fsdp")
    second_right = jnp.dot(
        model_side[:, :rank].astype(jnp.bfloat16),
        second_sign_mixer.astype(jnp.bfloat16),
        preferred_element_type=jnp.float32,
    )
    model_side = jnp.concatenate([second_right, model_side[:, rank:]], axis=1)
    model_side = lax.all_gather(model_side, "dp", axis=0, tiled=True)

    hidden_factors = jnp.concatenate(
        [adapter_second, sketch_hidden.astype(jnp.bfloat16).T], axis=0
    )

    def silu(v):
        return jax.nn.silu(v.astype(jnp.float32))

    def upstream(grad, group):
        return contract_last(grad, down_weight[group * span : (group + 1) * span])

    def sketched(scaled, group):
        return contract_last(scaled, hidden_factors[:, group * span : (group + 1) * span])

    total_a = total_b = total_c = total_d = 0.0
    neighbour = []
    for i in range(CHUNKS):
        up = upstream(grad_a, i)
        scaled = jnp.where(outer, up, up * silu(near[i])).astype(jnp.bfloat16)
        total_a = total_a + sketched(scaled, i)
        neighbour.append(lax.ppermute(scaled, "dp", inward))
    for i in range(CHUNKS):
        gate = jnp.where(outer, far_outer[i], far_inner[i])
        scaled = (upstream(grad_c, i) * silu(gate)).astype(jnp.bfloat16)
        total_c = total_c + sketched(scaled, i)
    for i in range(CHUNKS):
        up = upstream(grad_b, i) + jnp.where(outer, 0.0, neighbour[i].astype(jnp.float32))
        scaled = (up * silu(own[i])).astype(jnp.bfloat16)
        total_b = total_b + sketched(scaled, i)
        gate = jnp.where(outer, last_outer[i], last_inner[i])
        scaled = (upstream(grad_d, i) * silu(gate)).astype(jnp.bfloat16)
        total_d = total_d + sketched(scaled, i)

    total_a = jnp.where(outer, 0.0, total_a)
    low_pair = jnp.stack([jnp.where(z == 0, total_b, total_a), jnp.where(z == 0, total_a, total_b)])
    high_pair = jnp.stack([jnp.where(z == 2, total_b, total_a), jnp.where(z == 2, total_a, total_b)])
    others = jnp.stack([jnp.where(low, total_c, total_d), jnp.where(low, total_d, total_c)])
    sums = jnp.concatenate(
        [jnp.where(low, low_pair, others), jnp.where(low, others, high_pair)], axis=0
    )

    count = tokens // SEQ
    sums = sums.reshape(planes * count, SEQ, rank + K1)
    model_side = model_side.reshape(planes * count, SEQ, K2 + K1)
    back, left_hidden = sums[..., :rank], sums[..., rank:]
    second_right, left_model = model_side[..., :K2], model_side[..., K2:]
    projected = jnp.einsum(
        "esa,esb->eab", left_hidden, second_right, precision=lax.Precision.HIGHEST
    )
    crossed = jnp.einsum("esa,esr->ear", left_model, back, precision=lax.Precision.HIGHEST)
    projected = projected + jnp.einsum(
        "ear,rb->eab",
        crossed,
        mixer_first.astype(jnp.float32),
        precision=lax.Precision.HIGHEST,
    )
    projected = projected.reshape(planes, count, K1 * K2)
    projected = lax.all_to_all(projected, "dp", 0, 0, tiled=True)
    projected = lax.psum(jnp.sum(projected, axis=0), "fsdp")
    features = projected * lax.rsqrt(jnp.mean(projected * projected, axis=1, keepdims=True) + 1e-06)
    centre = jnp.sum(lax.all_gather(jnp.sum(features, axis=0), "dp"), axis=0) / (planes * count)
    scores = jnp.dot(features, centre, precision=lax.Precision.HIGHEST) / (
        K1 * K2 * jnp.sqrt(jnp.mean(centre * centre) + 1e-06)
    )
    return (features, scores)


def solution(mesh):
    placed = (
        P("dp", "fsdp"),
        P("dp", "fsdp"),
        P("dp", "fsdp"),
        P("fsdp", "dp"),
        P("fsdp", None),
        P(None, "fsdp"),
        P("fsdp", None),
        P("fsdp", None),
        P(),
        P(),
    )
    return jax.shard_map(
        body, mesh=mesh, in_specs=placed, out_specs=(P("dp", None), P("dp")), check_vma=False
    )
```
